32 devices in a mesh: side: 2 (over core), dev: 16 (over z, y, x).
Axes of the slice: x: 2, y: 2, z: 4, core: 2. Of those that a mesh axis runs over, the one named last changes fastest.
Arguments:
- out_gates: bfloat16 [512, 2048], P('dev'), may hold values from -6 to 6
- queries: bfloat16 [512, 2048], P('dev'), may hold values from -6 to 6
- keys_new: bfloat16 [512, 256], P('dev'), may hold values from -6 to 6
- values_new: bfloat16 [512, 256], P('dev'), may hold values from -6 to 6
- lengths: int32 [512], P('dev'), may hold values from 1 to 128, as said below
- page_table: int32 [512, 8], P('dev'), may hold values from 0 to 143, as said below
- cache_pool: bfloat16 [2304, 16, 512], P('dev'), may hold values from -1 to 1
- query_gain: float32 [256], replicated, may hold values from 0.25 to 1.75
- key_gain: float32 [256], replicated, may hold values from 0.25 to 1.75
- out_weight: bfloat16 [2048, 2048], replicated, may hold values from -0.125 to 0.125
- residual: bfloat16 [512, 2048], P('dev'), may hold values from -0.625 to 0.625
- post_gain: float32 [2048], replicated, may hold values from 0.25 to 1.75
- experts: int32 [512, 10], P('dev'), may hold values from 0 to 63, all different within a row; in each aligned block of 32 rows (0 to 31, 32 to 63, ...) at most 8 rows name the same one
- route_weights: float32 [512, 10], P('dev'), may hold values from 0.05 to 1
- gate_weight: bfloat16 [64, 2048, 256], P('dev'), may hold values from -0.125 to 0.125
- up_weight: bfloat16 [64, 2048, 256], P('dev'), may hold values from -0.125 to 0.125
- down_weight: bfloat16 [64, 256, 2048], P('dev'), may hold values from -0.375 to 0.375
- shared_gate: bfloat16 [2048, 256], replicated, may hold values from -0.125 to 0.125
- shared_up: bfloat16 [2048, 256], replicated, may hold values from -0.125 to 0.125
- shared_down: bfloat16 [256, 2048], replicated, may hold values from -0.375 to 0.375
- shared_mix: bfloat16 [2048], replicated, may hold values from -0.125 to 0.125
Outputs:
- layer_out: bfloat16 [512, 2048], P('dev', 'side')
The draws below stay inside these ranges and needn't reach their ends.
Inputs may be any that keep to these rules, and one draw needn't show every extreme that they name: Each row names 10 different experts; the rows of one device (aligned blocks of 32 rows) name one expert at most 8 times. A row's cache fills its first ceil(lengths / 16) page-table entries; in every device some row holds 128 tokens. `page_table`: indices are local to the row's device. The used entries of one device's rows name each of its 144 pages exactly once; unused entries name arbitrary pages.
All inputs are finite; a program needn't handle non-finite values.
Results may differ from the reference program's by a relative error of at most 0.024.
Values may be sent and summed in bfloat16 or wider, within the bound.
A program may use at most 128 MiB of HBM per device.

```python
import math
import jax
import jax.numpy as jnp
import numpy as np
from jax import lax

D = 2048
HD = 256
HQ = 8
FE = 256
SFE = 256
TOPK = 10
PAGE = 16
MAXP = 8
ROWS_DEV = 32
EXPERTS = 64
CAP = 8
POOL_DEV = 144
ROWS = 512
POOL = 2304
N_DEV = 16


def shared_pages(key):
    pairs = ROWS_DEV // 2
    first = jax.random.randint(jax.random.fold_in(key, 101), (N_DEV, pairs), 1, MAXP + 1)
    lead = jnp.arange(pairs, dtype=jnp.int32)[None, :] == 0
    first = jnp.where(lead, MAXP, first)
    count = jnp.stack([first, MAXP + 1 - first], axis=2).reshape(N_DEV, ROWS_DEV)
    offset = jax.random.randint(jax.random.fold_in(key, 102), (N_DEV, pairs, 2), 1, PAGE + 1)
    forced = lead[:, :, None] & (jnp.arange(2, dtype=jnp.int32)[None, None, :] == 0)
    offset = jnp.where(forced, PAGE, offset).reshape(N_DEV, ROWS_DEV)
    order_score = jax.random.randint(jax.random.fold_in(key, 103), (N_DEV, ROWS_DEV), 0, 1 << 20) * ROWS_DEV + jnp.arange(ROWS_DEV, dtype=jnp.int32)[None, :]
    order = jnp.argsort(order_score, axis=1)
    count = jnp.take_along_axis(count, order, axis=1)
    offset = jnp.take_along_axis(offset, order, axis=1)
    lengths = (count - 1) * PAGE + offset
    start = jnp.cumsum(count, axis=1) - count
    pool_score = jax.random.randint(jax.random.fold_in(key, 104), (N_DEV, POOL_DEV), 0, 1 << 20) * POOL_DEV + jnp.arange(POOL_DEV, dtype=jnp.int32)[None, :]
    pool_order = jnp.argsort(pool_score, axis=1).astype(jnp.int32)
    entry = jnp.arange(MAXP, dtype=jnp.int32)[None, None, :]
    position = jnp.minimum(start[:, :, None] + entry, POOL_DEV - 1).reshape(N_DEV, ROWS_DEV * MAXP)
    named = jnp.take_along_axis(pool_order, position, axis=1).reshape(N_DEV, ROWS_DEV, MAXP)
    spare = jax.random.randint(jax.random.fold_in(key, 105), (N_DEV, ROWS_DEV, MAXP), 0, POOL_DEV)
    table = jnp.where(entry < count[:, :, None], named, spare)
    return (lengths.reshape(ROWS_DEV * N_DEV).astype(jnp.int32), table.reshape(ROWS_DEV * N_DEV, MAXP).astype(jnp.int32))


def draw_lengths(key, part):
    both = shared_pages(key)
    return both[0]


def draw_page_table(key, part):
    both = shared_pages(key)
    return both[1]


def shard_levels(stream_key, shape, shards, least, largest):
    level = 1.0
    for axis_at, blocks in shards:
        draws = jax.random.uniform(jax.random.fold_in(jax.random.fold_in(stream_key, 6), axis_at), (blocks,), jnp.float32, least / len(shards), largest / len(shards))
        level = level * jnp.repeat(jnp.exp(draws), shape[axis_at] // blocks).reshape((-1,) + (1,) * (len(shape) - 1 - axis_at))
    return level


def routed_block(rng, own, number, rows, number_of, top, limit, skew):
    ranking = jax.random.permutation(rng, number_of)
    packed, usual = shares(number_of, rows * top, limit, skew, True), shares(number_of, rows * top, limit, skew, False)
    places = jnp.arange(number_of)

    def named(sizes, rotation):
        used = int((sizes > 0).sum())
        fixed = max(1, used // 4)
        passed = fixed + (places - fixed + rotation * (used - fixed)) % max(1, number_of - fixed)
        return jnp.zeros((number_of,), jnp.int32).at[ranking[jnp.where(places < fixed, places, passed)]].set(jnp.asarray(sizes, jnp.int32))

    sizes = jnp.where(number % 4 == 0, named(packed, number // 4), named(usual, number - number // 4 - 1))
    mixed = jax.random.permutation(jax.random.fold_in(own, 3), number_of)
    source_of, taker = mixed[0:number_of // 2 * 2:2], mixed[1:number_of // 2 * 2:2]
    room = jnp.minimum(sizes[source_of] - 1, limit - sizes[taker]) // 2
    room = jnp.where((source_of == ranking[0]) | (taker == ranking[0]) | (sizes[taker] == 0), 0, jnp.maximum(room, 0))
    passed = jax.random.randint(jax.random.fold_in(own, 4), (number_of // 2,), 0, 1 << 20) % (room + 1)
    sizes = sizes.at[source_of].add(-passed).at[taker].add(passed)
    members = jnp.searchsorted(jnp.cumsum(sizes), jnp.arange(rows * top), side="right").astype(jnp.int32)
    grid = members.reshape(top, rows).T
    grid = grid[jax.random.permutation(jax.random.fold_in(own, 1), rows)]
    rotation = jax.random.randint(jax.random.fold_in(own, 2), (rows, 1), 0, top)
    return jnp.take_along_axis(grid, (jnp.arange(top)[None, :] + rotation) % top, axis=1)


def shares(count, total, most, skew, full):
    weights = [(1 << 20) // math.isqrt(standing ** skew) + 1 for standing in range(1, count + 1)]
    largest = most if full else min(most, max(-(-total // count), total * weights[0] // sum(weights)))
    least = 1 if total - largest >= count - 1 else 0
    holding, spare = [largest] + [least] * (count - 1), total - largest - least * (count - 1)
    while spare > 0:
        movable = [i for i in range(1, count) if holding[i] < largest] or [i for i in range(1, count) if holding[i] < most]
        pool, budget = sum([weights[i] for i in movable]), spare
        for i in movable:
            addition = min(most - holding[i], max(1, budget * weights[i] // pool), spare)
            holding[i] = holding[i] + addition
            spare = spare - addition
    return np.array(holding)


def gaussian(own_key, extent, spread, reach, split=(), held_as=jnp.bfloat16):
    level = shard_levels(own_key, extent, split, -0.22, 0.18) if split else 1.0
    result = jax.random.normal(own_key, extent, jnp.float32) * spread * level
    return jnp.minimum(jnp.maximum(result, -reach), reach).astype(held_as)


def setup_inputs(seed: int = 0) -> dict:
    arg_keys = jax.random.split(jax.random.key(seed), 22)
    out_gates = gaussian(arg_keys[0], (ROWS, HQ * HD), 1.0, 6.0, ((0, 16),))
    queries = gaussian(arg_keys[1], (ROWS, HQ * HD), 1.0, 6.0, ((0, 16),))
    keys_new = gaussian(arg_keys[2], (ROWS, HD), 1.0, 6.0, ((0, 16),))
    values_new = gaussian(arg_keys[3], (ROWS, HD), 1.0, 6.0, ((0, 16),))
    lengths = draw_lengths(jax.random.fold_in(arg_keys[21], 71), 0)
    page_table = draw_page_table(jax.random.fold_in(arg_keys[21], 71), 0)
    cache_pool = jnp.clip(jax.random.uniform(arg_keys[6], (POOL, PAGE, 2 * HD), jnp.float32, -1.0, 1.0) * shard_levels(arg_keys[6], (POOL, PAGE, 2 * HD), ((0, 16),), -0.4, 0.0), -1.0, 1.0).astype(jnp.bfloat16)
    query_gain = jnp.clip(1.0 + 0.15 * jax.random.normal(arg_keys[7], (HD,), jnp.float32), 0.25, 1.75)
    key_gain = jnp.clip(1.0 + 0.15 * jax.random.normal(arg_keys[8], (HD,), jnp.float32), 0.25, 1.75)
    out_weight = gaussian(arg_keys[9], (HQ * HD, D), (HQ * HD) ** -0.5, 0.125)
    residual = gaussian(arg_keys[10], (ROWS, D), 0.1, 0.625, ((0, 16),))
    post_gain = jnp.clip(1.0 + 0.15 * jax.random.normal(arg_keys[11], (D,), jnp.float32), 0.25, 1.75)
    experts_keys = jax.random.split(jax.random.fold_in(arg_keys[12], 1), ROWS // ROWS_DEV)
    experts_turns = jax.random.permutation(jax.random.fold_in(arg_keys[12], 3), ROWS // ROWS_DEV)
    experts = jax.vmap(lambda own, number: routed_block(jax.random.fold_in(arg_keys[12], 2), own, number, ROWS_DEV, EXPERTS, TOPK, CAP, 2))(experts_keys, experts_turns).reshape((ROWS, TOPK))
    route_weights = jnp.clip(jnp.exp(math.log(1.0) - 2.9957323 * jax.random.uniform(arg_keys[13], (ROWS, TOPK), jnp.float32) ** shard_levels(arg_keys[13], (ROWS, TOPK), ((0, 16),), -0.2, 0.2)), 0.05, 1.0)
    gate_weight = gaussian(arg_keys[14], (EXPERTS, D, FE), D ** -0.5, 0.125, ((0, 16),))
    up_weight = gaussian(arg_keys[15], (EXPERTS, D, FE), D ** -0.5, 0.125, ((0, 16),))
    down_weight = gaussian(arg_keys[16], (EXPERTS, FE, D), FE ** -0.5, 0.375, ((0, 16),))
    shared_gate = gaussian(arg_keys[17], (D, SFE), D ** -0.5, 0.125)
    shared_up = gaussian(arg_keys[18], (D, SFE), D ** -0.5, 0.125)
    shared_down = gaussian(arg_keys[19], (SFE, D), SFE ** -0.5, 0.375)
    shared_mix = gaussian(arg_keys[20], (D,), D ** -0.5, 0.125)
    return dict(out_gates=out_gates, queries=queries, keys_new=keys_new, values_new=values_new, lengths=lengths, page_table=page_table, cache_pool=cache_pool, query_gain=query_gain, key_gain=key_gain, out_weight=out_weight, residual=residual, post_gain=post_gain, experts=experts, route_weights=route_weights, gate_weight=gate_weight, up_weight=up_weight, down_weight=down_weight, shared_gate=shared_gate, shared_up=shared_up, shared_down=shared_down, shared_mix=shared_mix)


eps = 1e-06

def rms_scale(values, gain):
    wide = values.astype(jnp.float32)
    return wide * lax.rsqrt(lax.optimization_barrier(jnp.mean(wide * wide, axis=-1, keepdims=True)) + eps) * gain.astype(jnp.float32)

def reference(out_gates, queries, keys_new, values_new, lengths, page_table, cache_pool, query_gain, key_gain, out_weight, residual, post_gain, experts, route_weights, gate_weight, up_weight, down_weight, shared_gate, shared_up, shared_down, shared_mix):
    scale = HD ** (-0.5)

    def one_device(block):
        gates_in, queries_in, keys_in, values_in, lengths_in, table_in, pool_in = block
        rows = queries_in.shape[0]
        query_normed = rms_scale(queries_in.reshape(rows, HQ, HD), query_gain).astype(jnp.bfloat16)
        key_normed = rms_scale(keys_in, key_gain).astype(jnp.bfloat16)
        pages = pool_in[table_in].reshape(rows, MAXP * PAGE, 2 * HD)
        cached_keys = pages[:, :, :HD].astype(jnp.float32)
        cached_values = pages[:, :, HD:].astype(jnp.float32)
        query_wide = query_normed.astype(jnp.float32)
        scores = jnp.einsum('rhd,rtd->rht', query_wide, cached_keys) * scale
        own = jnp.einsum('rhd,rd->rh', query_wide, key_normed.astype(jnp.float32)) * scale
        valid = jnp.arange(MAXP * PAGE, dtype=jnp.int32)[None, None, :] < lengths_in[:, None, None]
        weights = jnp.where(valid, jnp.exp(scores), 0.0)
        own_weight = jnp.exp(own)
        total = lax.optimization_barrier(jnp.sum(weights, axis=2)) + own_weight
        probs = (weights / total[:, :, None]).astype(jnp.bfloat16)
        own_prob = (own_weight / total).astype(jnp.bfloat16)
        mixed = jnp.einsum('rht,rtd->rhd', probs.astype(jnp.float32), cached_values)
        mixed = mixed + own_prob.astype(jnp.float32)[:, :, None] * values_in.astype(jnp.float32)[:, None, :]
        gated = mixed * jax.nn.sigmoid(gates_in.reshape(rows, HQ, HD).astype(jnp.float32))
        return gated.reshape(rows, HQ * HD).astype(jnp.bfloat16)
    blocks = (out_gates.reshape(N_DEV, ROWS_DEV, HQ * HD), queries.reshape(N_DEV, ROWS_DEV, HQ * HD), keys_new.reshape(N_DEV, ROWS_DEV, HD), values_new.reshape(N_DEV, ROWS_DEV, HD), lengths.reshape(N_DEV, ROWS_DEV), page_table.reshape(N_DEV, ROWS_DEV, MAXP), cache_pool.reshape(N_DEV, POOL_DEV, PAGE, 2 * HD))
    attended = lax.map(one_device, blocks).reshape(ROWS, HQ * HD)
    projected = jnp.dot(attended, out_weight, preferred_element_type=jnp.float32)
    hidden = (residual.astype(jnp.float32) + projected).astype(jnp.bfloat16)
    normed = rms_scale(hidden, post_gain).astype(jnp.bfloat16)
    slots_each = N_DEV * CAP
    flat = experts.reshape(-1).astype(jnp.int32)
    onehot = (flat[:, None] == jnp.arange(EXPERTS, dtype=jnp.int32)[None, :]).astype(jnp.int32)
    rank = lax.optimization_barrier(jnp.sum((jnp.cumsum(onehot, axis=0) - 1) * onehot, axis=1)).astype(jnp.int32)
    slot = (flat * slots_each + rank).astype(jnp.int32)
    source = jnp.repeat(jnp.arange(ROWS, dtype=jnp.int32), TOPK)
    buffer = jnp.zeros((EXPERTS * slots_each, D), jnp.bfloat16).at[slot].set(normed[source])

    def run_expert(item):
        rows_in, gate_in, up_in, down_in = item
        gate_val = jnp.dot(rows_in, gate_in, preferred_element_type=jnp.float32)
        up_val = jnp.dot(rows_in, up_in, preferred_element_type=jnp.float32)
        inner = (jax.nn.silu(gate_val) * up_val).astype(jnp.bfloat16)
        return jnp.dot(inner, down_in, preferred_element_type=jnp.float32).astype(jnp.bfloat16)
    results = lax.map(run_expert, (buffer.reshape(EXPERTS, slots_each, D), gate_weight, up_weight, down_weight))
    picked = results.reshape(EXPERTS * slots_each, D)[slot].reshape(ROWS, TOPK, D)
    share = route_weights / lax.optimization_barrier(jnp.sum(route_weights, axis=1, keepdims=True))
    routed = jnp.einsum('rk,rkd->rd', share, picked.astype(jnp.float32))
    shared_gate_val = jnp.dot(normed, shared_gate, preferred_element_type=jnp.float32)
    shared_up_val = jnp.dot(normed, shared_up, preferred_element_type=jnp.float32)
    shared_inner = (jax.nn.silu(shared_gate_val) * shared_up_val).astype(jnp.bfloat16)
    shared_out = jnp.dot(shared_inner, shared_down, preferred_element_type=jnp.float32)
    shared_weight = jax.nn.sigmoid(jnp.dot(normed, shared_mix, preferred_element_type=jnp.float32))
    total_out = hidden.astype(jnp.float32) + routed + shared_weight[:, None] * shared_out
    return total_out.astype(jnp.bfloat16)
```

```python
import functools

import jax
import jax.numpy as jnp
from jax import lax
from jax.experimental import pallas as pl
from jax.experimental.pallas import tpu as pltpu
from jax.sharding import PartitionSpec as P

eps = 1e-06
MESH = pl.DeviceIdType.MESH
F32 = jnp.float32
BF16 = jnp.bfloat16


def rms_scale(wide, gain):
    return wide * lax.rsqrt(jnp.mean(wide * wide, axis=-1, keepdims=True) + eps) * gain


def sigmoid(value):
    return 1.0 / (1.0 + jnp.exp(-value))


def dot(left, right):
    return jnp.dot(left, right, preferred_element_type=F32)


OUT_CHUNKS = 4


def kernel(
    planes,
    gates_h,
    queries_h,
    keys_h,
    values_h,
    lengths_h,
    table_h,
    pool_h,
    query_gain_h,
    key_gain_h,
    out_weight_h,
    residual_h,
    post_gain_h,
    experts_h,
    route_h,
    gate_weight_h,
    up_weight_h,
    down_weight_h,
    shared_gate_h,
    shared_up_h,
    shared_down_h,
    shared_mix_h,
    out_ref,
    gates,
    queries,
    keys,
    values,
    lengths,
    table,
    pool,
    query_gain,
    key_gain,
    out_weight,
    residual,
    post_gain,
    experts,
    route,
    gate_weight,
    up_weight,
    down_weight,
    shared_gate,
    shared_up,
    shared_down,
    shared_mix,
    gathered,
    select,
    partial,
    diag_in,
    x_in,
    y_in,
    plane_sum,
    z_in,
    base,
    base_out,
    base_in,
    load_sem,
    z_send,
    z_recv,
    x_send,
    x_recv,
    y_send,
    y_recv,
    da_send,
    da_recv,
    db_send,
    db_recv,
    ra_send,
    ra_recv,
    rb_send,
    rb_recv,
    rx_send,
    rx_recv,
    ry_send,
    ry_recv,
    rz_send,
    rz_recv,
    side_sem,
):
    side = lax.axis_index("side")
    dev = lax.axis_index("dev")
    other = 1 - side
    column = lax.rem(dev, 4)
    zi = dev // 4
    x_bit = lax.rem(dev, 2)
    y_bit = lax.rem(dev // 2, 2)
    x_col = column + 1 - 2 * x_bit
    y_col = column + 2 - 4 * y_bit
    d_col = 3 - column
    x_dev = zi * 4 + x_col
    y_dev = zi * 4 + y_col

    rows = queries.shape[0]
    width = residual.shape[1]
    half = width // 2
    wide = gathered.shape[2]
    head_dim = keys.shape[1]
    heads = queries.shape[1] // head_dim
    first = pl.multiple_of(side * rows, rows)

    loads = []

    def load(source, target):
        copy = pltpu.make_async_copy(source, target, load_sem.at[len(loads)])
        copy.start()
        loads.append(copy)
        return copy

    mine = pl.ds(first, rows)
    early = [
        load(queries_h.at[mine], queries),
        load(query_gain_h, query_gain),
        load(lengths_h, lengths),
        load(table_h.at[mine], table),
        load(pool_h, pool),
        load(keys_h.at[mine], keys),
        load(key_gain_h, key_gain),
        load(values_h.at[mine], values),
        load(gates_h.at[mine], gates),
    ]
    step = out_weight.shape[0] // OUT_CHUNKS
    out_loads = [
        load(out_weight_h.at[pl.ds(i * step, step)], out_weight.at[pl.ds(i * step, step)])
        for i in range(OUT_CHUNKS)
    ]
    norm_loads = [
        load(residual_h.at[mine], residual),
        load(post_gain_h, post_gain),
        load(experts_h.at[mine], experts),
        load(route_h.at[mine], route),
    ]
    shared_loads = [
        load(shared_gate_h, shared_gate),
        load(shared_up_h, shared_up),
        load(shared_down_h, shared_down),
        load(shared_mix_h, shared_mix),
    ]
    expert_loads = [
        load(source.at[i], target.at[i])
        for source, target in (
            (gate_weight_h, gate_weight),
            (up_weight_h, up_weight),
            (down_weight_h, down_weight),
        )
        for i in range(gate_weight.shape[0])
    ]

    barrier = pltpu.get_barrier_semaphore()

    def greet(to_side, to_dev):
        pl.semaphore_signal(barrier, inc=1, device_id=(to_side, to_dev), device_id_type=MESH)

    greet(other, dev)
    greet(side, x_dev)
    greet(side, y_dev)
    for k in range(1, planes):
        peer = lax.rem(zi + k, planes) * 4 + column
        greet(side, peer)
        greet(other, peer)

    for copy in early:
        copy.wait()
    tokens = pool.shape[0] * pool.shape[1]
    page = pool.shape[1]
    lane_row = lax.broadcasted_iota(jnp.int32, (rows, lengths.shape[1]), 1)
    sub_row = lax.broadcasted_iota(jnp.int32, (rows, lengths.shape[1]), 0) + first
    length_col = jnp.sum(jnp.where(lane_row == sub_row, lengths[...], 0), axis=1, keepdims=True)
    token = lax.broadcasted_iota(jnp.int32, (rows, tokens), 1)
    token_page = token // page
    token_at = token - token_page * page
    table_val = table[...]
    limit = jnp.zeros((rows, tokens), jnp.int32)
    for j in range(table.shape[1]):
        left = length_col - page * j
        named = jnp.where(left > 0, table_val[:, j : j + 1], -1)
        limit = jnp.where(token_page == named, left, limit)
    valid = jnp.where(limit > token_at, 1.0, 0.0)
    valid = jnp.concatenate([valid] * heads, axis=0)

    def head(value, h):
        return value[:, h * head_dim : (h + 1) * head_dim]

    queries_val = queries[...].astype(F32)
    query_parts = [
        rms_scale(head(queries_val, h), query_gain[...]).astype(BF16) for h in range(heads)
    ]
    key_normed = rms_scale(keys[...].astype(F32), key_gain[...]).astype(BF16).astype(F32)
    own = jnp.concatenate(
        [jnp.sum(q.astype(F32) * key_normed, axis=1, keepdims=True) for q in query_parts], axis=0
    )
    query_all = jnp.concatenate(query_parts, axis=0)
    scale = head_dim ** (-0.5)
    cached_keys = pool[:, :, :head_dim].reshape(tokens, head_dim)
    scores = lax.dot_general(
        query_all, cached_keys, (((1,), (1,)), ((), ())), preferred_element_type=F32
    )
    weights = jnp.where(valid > 0.0, jnp.exp(scores * scale), 0.0)
    own_weight = jnp.exp(own * scale)
    total = jnp.sum(weights, axis=1, keepdims=True) + own_weight
    cached_values = pool[:, :, head_dim:].reshape(tokens, head_dim)
    mixed = dot(weights.astype(BF16), cached_values)
    values_all = jnp.concatenate([values[...].astype(F32)] * heads, axis=0)
    mixed = (mixed + own_weight * values_all) / total
    attended = jnp.concatenate(
        [
            (
                mixed[h * rows : (h + 1) * rows]
                * sigmoid(gates[:, h * head_dim : (h + 1) * head_dim].astype(F32))
            ).astype(BF16)
            for h in range(heads)
        ],
        axis=1,
    )

    projected = jnp.zeros((rows, width), F32)
    for i, copy in enumerate(out_loads):
        copy.wait()
        projected = projected + dot(
            attended[:, i * step : (i + 1) * step], out_weight[i * step : (i + 1) * step, :]
        )
    for copy in norm_loads:
        copy.wait()
    hidden = (residual[...].astype(F32) + projected).astype(BF16).astype(F32)
    normed = rms_scale(hidden, post_gain[...]).astype(BF16)

    route_val = route[...]
    share = route_val / jnp.sum(route_val, axis=1, keepdims=True)
    chosen = experts[...]
    terms = wide - width
    experts_all = terms // 2
    place = lax.broadcasted_iota(jnp.int32, (rows, terms), 1)
    expert_at = lax.rem(place, experts_all)
    spread = jnp.zeros((rows, terms), F32)
    for k in range(experts.shape[1]):
        spread = spread + jnp.where(expert_at == chosen[:, k : k + 1], share[:, k : k + 1], 0.0)
    leading = spread.astype(BF16).astype(F32)
    spread = jnp.where(place < experts_all, leading, spread - leading).astype(BF16)
    gathered[dev] = jnp.concatenate([normed, spread], axis=1)

    pl.semaphore_wait(barrier, 3 + 2 * (planes - 1))

    def remote(source, target, send, recv, to_side, to_dev):
        return pltpu.make_async_remote_copy(
            src_ref=source,
            dst_ref=target,
            send_sem=send,
            recv_sem=recv,
            device_id=(to_side, to_dev),
            device_id_type=MESH,
        )

    def plane(k):
        return lax.rem(zi - k + planes, planes)

    part_a = pl.ds(0, half)
    part_b = pl.ds(half, wide - half)
    out_a = pl.ds(0, half)
    out_b = pl.ds(half, half)

    def send_z(k):
        peer = lax.rem(zi + k, planes) * 4 + column
        return remote(
            gathered.at[dev], gathered.at[dev], z_send.at[k], z_recv.at[k], side, peer
        )

    def send_x(k):
        block = gathered.at[plane(k) * 4 + column]
        return remote(block, block, x_send.at[k], x_recv.at[k], side, x_dev)

    def send_y(k):
        block = gathered.at[plane(k) * 4 + column]
        return remote(block, block, y_send.at[k], y_recv.at[k], side, y_dev)

    def send_da(k):
        block = gathered.at[plane(k) * 4 + x_col, :, part_a]
        return remote(block, block, da_send.at[k], da_recv.at[k], side, y_dev)

    def send_db(k):
        block = gathered.at[plane(k) * 4 + y_col, :, part_b]
        return remote(block, block, db_send.at[k], db_recv.at[k], side, x_dev)

    def send_ra(k):
        return remote(
            partial.at[k, d_col, :, out_a],
            diag_in.at[k, :, out_a],
            ra_send.at[k],
            ra_recv.at[k],
            side,
            x_dev,
        )

    def send_rb(k):
        return remote(
            partial.at[k, d_col, :, out_b],
            diag_in.at[k, :, out_b],
            rb_send.at[k],
            rb_recv.at[k],
            side,
            y_dev,
        )

    def send_rx(k):
        return remote(
            partial.at[k, x_col], x_in.at[k], rx_send.at[k], rx_recv.at[k], side, x_dev
        )

    def send_ry(k):
        return remote(
            partial.at[k, y_col], y_in.at[k], ry_send.at[k], ry_recv.at[k], side, y_dev
        )

    def send_rz(k, to_side):
        columns = pl.ds(pl.multiple_of(to_side * half, half), half)
        return remote(
            plane_sum.at[k, :, columns],
            z_in.at[k, side],
            rz_send.at[k, to_side],
            rz_recv.at[k, side],
            to_side,
            plane(k) * 4 + column,
        )

    def wait_rz(k, from_side):
        columns = pl.ds(pl.multiple_of(side * half, half), half)
        remote(
            plane_sum.at[k, :, columns],
            z_in.at[k, from_side],
            rz_send.at[k, side],
            rz_recv.at[k, from_side],
            side,
            lax.rem(zi + k, planes) * 4 + column,
        ).wait_recv()

    send_x(0).start()
    send_y(0).start()
    for k in range(1, planes):
        send_z(k).start()

    for copy in shared_loads:
        copy.wait()
    gate_val = dot(normed, shared_gate[...])
    up_val = dot(normed, shared_up[...])
    inner = (gate_val * sigmoid(gate_val) * up_val).astype(BF16)
    mix = jnp.sum(normed.astype(F32) * shared_mix[...].astype(F32), axis=1, keepdims=True)
    base[...] = hidden + sigmoid(mix) * dot(inner, shared_down[...])

    local = gate_weight.shape[0]
    hidden_units = gate_weight.shape[2]
    term = lax.broadcasted_iota(jnp.int32, select.shape, 0)
    unit = lax.broadcasted_iota(jnp.int32, select.shape, 1)
    wanted = dev * local + unit // hidden_units
    select[...] = jnp.where(lax.rem(term, experts_all) == wanted, 1.0, 0.0).astype(BF16)

    for k in range(1, planes):
        send_z(k).wait_recv()
        send_x(k).start()
        send_y(k).start()
    for copy in expert_loads:
        copy.wait()

    def forward(k):
        send_x(k).wait_recv()
        send_da(k).start()
        send_y(k).wait_recv()
        send_db(k).start()

    def serve(k):
        send_da(k).wait_recv()
        send_db(k).wait_recv()
        at = pl.ds(pl.multiple_of(plane(k) * 4, 4), 4)
        block = gathered[at].reshape(4 * rows, wide)
        taken = block[:, :width]
        shares = dot(block[:, width:], select[...])
        inners = []
        for i in range(local):
            gate_part = dot(taken, gate_weight[i])
            up_part = dot(taken, up_weight[i])
            weight = shares[:, i * hidden_units : (i + 1) * hidden_units]
            inners.append((gate_part * sigmoid(gate_part) * up_part * weight).astype(BF16))
        inner_all = jnp.concatenate(inners, axis=1)
        down = down_weight[...].reshape(local * hidden_units, width)
        result = dot(inner_all, down).astype(BF16)
        partial[k] = result.reshape(4, rows, width)
        send_ra(k).start()
        send_rb(k).start()

    def reduce_diag(k):
        send_ra(k).wait_recv()
        partial[k, y_col, :, :half] = (
            partial[k, y_col, :, :half].astype(F32) + diag_in[k, :, :half].astype(F32)
        ).astype(BF16)
        send_ry(k).start()
        send_rb(k).wait_recv()
        partial[k, x_col, :, half:] = (
            partial[k, x_col, :, half:].astype(F32) + diag_in[k, :, half:].astype(F32)
        ).astype(BF16)
        send_rx(k).start()

    def reduce_plane(k):
        send_rx(k).wait_recv()
        send_ry(k).wait_recv()
        summed = (
            partial[k, column].astype(F32) + x_in[k].astype(F32) + y_in[k].astype(F32)
        )

        @pl.when(k > 0)
        def _():
            plane_sum[k] = summed.astype(BF16)
            send_rz(k, 0).start()
            send_rz(k, 1).start()

        @pl.when(k == 0)
        def _():
            base[...] = base[...] + summed
            base_out[...] = base[:, pl.ds(pl.multiple_of(other * half, half), half)]
            send_base().start()

    def send_base():
        return remote(base_out, base_in, side_sem.at[0], side_sem.at[1], other, dev)

    forward(0)

    def turn(k, carry):
        @pl.when(k + 1 < planes)
        def _():
            forward(k + 1)

        @pl.when(k < planes)
        def _():
            serve(k)

        @pl.when((k >= 1) & (k <= planes))
        def _():
            reduce_diag(k - 1)

        @pl.when(k >= 2)
        def _():
            reduce_plane(k - 2)

        return carry

    lax.fori_loop(0, planes + 2, turn, 0)

    send_base().wait_recv()
    own_rows = base[:, pl.ds(pl.multiple_of(side * half, half), half)]
    other_rows = base_in[...]
    for k in range(1, planes):
        wait_rz(k, side)
        own_rows = own_rows + z_in[k, side].astype(F32)
        wait_rz(k, other)
        other_rows = other_rows + z_in[k, other].astype(F32)
    out_ref[pl.ds(first, rows), :] = own_rows.astype(BF16)
    out_ref[pl.ds(pl.multiple_of(other * rows, rows), rows), :] = other_rows.astype(BF16)

    def drain(k, carry):
        for send in (send_x, send_y, send_da, send_db, send_ra, send_rb, send_rx, send_ry):
            send(k).wait_send()

        @pl.when(k > 0)
        def _():
            send_z(k).wait_send()
            send_rz(k, 0).wait_send()
            send_rz(k, 1).wait_send()

        return carry

    lax.fori_loop(0, planes, drain, 0)
    send_base().wait_send()


def on_device(
    out_gates,
    queries,
    keys_new,
    values_new,
    lengths,
    page_table,
    cache_pool,
    query_gain,
    key_gain,
    out_weight,
    residual,
    post_gain,
    experts,
    route_weights,
    gate_weight,
    up_weight,
    down_weight,
    shared_gate,
    shared_up,
    shared_down,
    shared_mix,
):
    n_dev = lax.axis_size("dev")
    planes = n_dev // 4
    rows_dev, width = residual.shape
    rows = rows_dev // 2
    half = width // 2
    local, _, hidden_units = gate_weight.shape
    terms = 2 * local * n_dev
    operands = (
        out_gates,
        queries,
        keys_new,
        values_new,
        lengths.reshape(1, -1),
        page_table,
        cache_pool,
        query_gain.reshape(1, -1),
        key_gain.reshape(1, -1),
        out_weight,
        residual,
        post_gain.reshape(1, -1),
        experts,
        route_weights,
        gate_weight,
        up_weight,
        down_weight,
        shared_gate,
        shared_up,
        shared_down,
        shared_mix.reshape(1, -1),
    )
    by_row = (0, 1, 2, 3, 5, 10, 12, 13)
    held = [
        pltpu.VMEM(((rows,) + value.shape[1:]) if i in by_row else value.shape, value.dtype)
        for i, value in enumerate(operands)
    ]
    loads = len(operands) - 4 + OUT_CHUNKS + 3 * local
    per_plane = pltpu.SemaphoreType.DMA((planes,))
    per_side = pltpu.SemaphoreType.DMA((planes, 2))
    flops = 2 * width * (
        width * rows + 3 * hidden_units * rows * (n_dev * local + 1)
    )
    return pl.pallas_call(
        functools.partial(kernel, planes),
        out_shape=jax.ShapeDtypeStruct((rows_dev, half), BF16),
        in_specs=[pl.BlockSpec(memory_space=pl.ANY)] * len(operands),
        out_specs=pl.BlockSpec(memory_space=pltpu.VMEM),
        scratch_shapes=held
        + [
            pltpu.VMEM((n_dev, rows, width + terms), BF16),
            pltpu.VMEM((terms, local * hidden_units), BF16),
            pltpu.VMEM((planes, 4, rows, width), BF16),
            pltpu.VMEM((planes, rows, width), BF16),
            pltpu.VMEM((planes, rows, width), BF16),
            pltpu.VMEM((planes, rows, width), BF16),
            pltpu.VMEM((planes, rows, width), BF16),
            pltpu.VMEM((planes, 2, rows, half), BF16),
            pltpu.VMEM((rows, width), F32),
            pltpu.VMEM((rows, half), F32),
            pltpu.VMEM((rows, half), F32),
            pltpu.SemaphoreType.DMA((loads,)),
        ]
        + [per_plane] * 18
        + [per_side] * 2
        + [pltpu.SemaphoreType.DMA((2,))],
        compiler_params=pltpu.CompilerParams(
            collective_id=0, has_side_effects=True, vmem_limit_bytes=56 * 1024 * 1024
        ),
        cost_estimate=pl.CostEstimate(
            flops=flops, bytes_accessed=27 * 1024 * 1024, transcendentals=1024 * 1024
        ),
    )(*operands)


def solution(mesh):
    placed = (
        P("dev", None),
        P("dev", None),
        P("dev", None),
        P("dev", None),
        P("dev"),
        P("dev", None),
        P("dev", None, None),
        P(),
        P(),
        P(),
        P("dev", None),
        P(),
        P("dev", None),
        P("dev", None),
        P("dev", None, None),
        P("dev", None, None),
        P("dev", None, None),
        P(),
        P(),
        P(),
        P(),
    )
    return jax.shard_map(
        on_device, mesh=mesh, in_specs=placed, out_specs=P("dev", "side"), check_vma=False
    )
```

```python
import functools

import jax
import jax.numpy as jnp
from jax import lax
from jax.experimental import pallas as pl
from jax.experimental.pallas import tpu as pltpu
from jax.sharding import PartitionSpec as P

eps = 1e-06
MESH = pl.DeviceIdType.MESH
F32 = jnp.float32
BF16 = jnp.bfloat16


def rms_scale(wide, gain):
    return wide * lax.rsqrt(jnp.mean(wide * wide, axis=-1, keepdims=True) + eps) * gain


def sigmoid(value):
    return 1.0 / (1.0 + jnp.exp(-value))


def dot(left, right):
    return jnp.dot(left, right, preferred_element_type=F32)


def quotient(value, by):
    if by & (by - 1) == 0:
        return lax.shift_right_logical(value, jnp.full_like(value, by.bit_length() - 1))
    return value // by


def remainder(value, by):
    if by & (by - 1) == 0:
        return value & (by - 1)
    return lax.rem(value, by)


OUT_CHUNKS = 4


def kernel(
    planes,
    gates_h,
    queries_h,
    keys_h,
    values_h,
    lengths_h,
    table_h,
    pool_h,
    query_gain_h,
    key_gain_h,
    out_weight_h,
    residual_h,
    post_gain_h,
    experts_h,
    route_h,
    gate_weight_h,
    up_weight_h,
    down_weight_h,
    shared_gate_h,
    shared_up_h,
    shared_down_h,
    shared_mix_h,
    out_ref,
    gates,
    queries,
    keys,
    values,
    lengths,
    table,
    pool,
    query_gain,
    key_gain,
    out_weight,
    residual,
    post_gain,
    experts,
    route,
    gate_weight,
    up_weight,
    down_weight,
    shared_gate,
    shared_up,
    shared_down,
    shared_mix,
    gathered,
    select,
    partial,
    diag_in,
    x_in,
    y_in,
    plane_sum,
    z_in,
    base,
    base_out,
    base_in,
    load_sem,
    z_send,
    z_recv,
    x_send,
    x_recv,
    y_send,
    y_recv,
    da_send,
    da_recv,
    db_send,
    db_recv,
    ra_send,
    ra_recv,
    rb_send,
    rb_recv,
    rx_send,
    rx_recv,
    ry_send,
    ry_recv,
    rz_send,
    rz_recv,
    side_sem,
):
    side = lax.axis_index("side")
    dev = lax.axis_index("dev")
    other = 1 - side
    column = lax.rem(dev, 4)
    zi = dev // 4
    x_bit = lax.rem(dev, 2)
    y_bit = lax.rem(dev // 2, 2)
    x_col = column + 1 - 2 * x_bit
    y_col = column + 2 - 4 * y_bit
    d_col = 3 - column
    x_dev = zi * 4 + x_col
    y_dev = zi * 4 + y_col

    rows = queries.shape[0]
    width = residual.shape[1]
    half = width // 2
    wide = gathered.shape[2]
    head_dim = keys.shape[1]
    heads = queries.shape[1] // head_dim
    first = pl.multiple_of(side * rows, rows)

    loads = []

    def load(source, target):
        copy = pltpu.make_async_copy(source, target, load_sem.at[len(loads)])
        copy.start()
        loads.append(copy)
        return copy

    mine = pl.ds(first, rows)
    small_loads = [
        load(queries_h.at[mine], queries),
        load(query_gain_h, query_gain),
        load(keys_h.at[mine], keys),
        load(key_gain_h, key_gain),
        load(lengths_h, lengths),
        load(table_h, table),
        load(experts_h, experts),
        load(route_h, route),
    ]
    pool_load = load(pool_h, pool)
    late_loads = [
        load(values_h.at[mine], values),
        load(gates_h.at[mine], gates),
        load(residual_h.at[mine], residual),
        load(post_gain_h, post_gain),
    ]
    step = out_weight.shape[0] // OUT_CHUNKS
    out_loads = [
        load(out_weight_h.at[pl.ds(i * step, step)], out_weight.at[pl.ds(i * step, step)])
        for i in range(OUT_CHUNKS)
    ]

    barrier = pltpu.get_barrier_semaphore()

    def greet(to_side, to_dev):
        pl.semaphore_signal(barrier, inc=1, device_id=(to_side, to_dev), device_id_type=MESH)

    greet(other, dev)
    greet(side, x_dev)
    greet(side, y_dev)
    for k in range(1, planes):
        peer = lax.rem(zi + k, planes) * 4 + column
        greet(side, peer)
        greet(other, peer)

    for copy in small_loads:
        copy.wait()

    lane_row = lax.broadcasted_iota(jnp.int32, (rows, lengths.shape[1]), 1)
    sub_row = lax.broadcasted_iota(jnp.int32, (rows, lengths.shape[1]), 0) + first
    picked = lane_row == sub_row

    def as_column(line):
        return jnp.sum(jnp.where(picked, line, jnp.zeros_like(line)), axis=1, keepdims=True)

    width_terms = wide - width
    experts_all = width_terms // 2
    route_val = route[...]
    share = route_val / jnp.sum(route_val, axis=0, keepdims=True)
    chosen = experts[...]
    place = lax.broadcasted_iota(jnp.int32, (rows, width_terms), 1)
    expert_at = remainder(place, experts_all)
    spread = jnp.zeros((rows, width_terms), F32)
    for k in range(experts.shape[0]):
        spread = spread + jnp.where(
            expert_at == as_column(chosen[k : k + 1]), as_column(share[k : k + 1]), 0.0
        )
    leading = spread.astype(BF16).astype(F32)
    spread = jnp.where(place < experts_all, leading, spread - leading).astype(BF16)

    tokens = pool.shape[0] * pool.shape[1]
    page = pool.shape[1]
    length_col = as_column(lengths[...])
    token = lax.broadcasted_iota(jnp.int32, (rows, tokens), 1)
    token_page = quotient(token, page)
    token_at = remainder(token, page)
    table_val = table[...]
    limit = jnp.zeros((rows, tokens), jnp.int32)
    for j in range(table.shape[0]):
        left = length_col - page * j
        named = jnp.where(left > 0, as_column(table_val[j : j + 1]), -1)
        limit = jnp.where(token_page == named, left, limit)
    valid = jnp.where(limit > token_at, 1.0, 0.0)
    valid = jnp.concatenate([valid] * heads, axis=0)

    def head(value, h):
        return value[:, h * head_dim : (h + 1) * head_dim]

    queries_val = queries[...].astype(F32)
    query_parts = [
        rms_scale(head(queries_val, h), query_gain[...]).astype(BF16) for h in range(heads)
    ]
    key_normed = rms_scale(keys[...].astype(F32), key_gain[...]).astype(BF16).astype(F32)
    own = jnp.concatenate(
        [jnp.sum(q.astype(F32) * key_normed, axis=1, keepdims=True) for q in query_parts], axis=0
    )
    query_all = jnp.concatenate(query_parts, axis=0)
    scale = head_dim ** (-0.5)
    pool_load.wait()
    cached_keys = pool[:, :, :head_dim].reshape(tokens, head_dim)
    shared_loads = [
        load(shared_gate_h, shared_gate),
        load(shared_up_h, shared_up),
        load(shared_down_h, shared_down),
        load(shared_mix_h, shared_mix),
    ]
    expert_loads = [
        load(source.at[i], target.at[i])
        for source, target in (
            (gate_weight_h, gate_weight),
            (up_weight_h, up_weight),
            (down_weight_h, down_weight),
        )
        for i in range(gate_weight.shape[0])
    ]
    scores = lax.dot_general(
        query_all, cached_keys, (((1,), (1,)), ((), ())), preferred_element_type=F32
    )
    weights = jnp.where(valid > 0.0, jnp.exp(scores * scale), 0.0)
    own_weight = jnp.exp(own * scale)
    total = jnp.sum(weights, axis=1, keepdims=True) + own_weight
    cached_values = pool[:, :, head_dim:].reshape(tokens, head_dim)
    mixed = dot(weights.astype(BF16), cached_values)
    for copy in late_loads:
        copy.wait()
    values_all = jnp.concatenate([values[...].astype(F32)] * heads, axis=0)
    mixed = (mixed + own_weight * values_all) / total
    attended = jnp.concatenate(
        [
            (
                mixed[h * rows : (h + 1) * rows]
                * sigmoid(gates[:, h * head_dim : (h + 1) * head_dim].astype(F32))
            ).astype(BF16)
            for h in range(heads)
        ],
        axis=1,
    )

    local = gate_weight.shape[0]
    hidden_units = gate_weight.shape[2]
    term = lax.broadcasted_iota(jnp.int32, (select.shape[0], 1), 0)
    unit = lax.broadcasted_iota(jnp.int32, (1, select.shape[1]), 1)
    wanted = dev * local + quotient(unit, hidden_units)
    select[...] = jnp.where(remainder(term, experts_all) == wanted, 1.0, 0.0).astype(BF16)

    projected = jnp.zeros((rows, width), F32)
    for i, copy in enumerate(out_loads):
        copy.wait()
        projected = projected + dot(
            attended[:, i * step : (i + 1) * step], out_weight[i * step : (i + 1) * step, :]
        )
    hidden = (residual[...].astype(F32) + projected).astype(BF16).astype(F32)
    normed = rms_scale(hidden, post_gain[...]).astype(BF16)

    gathered[dev] = jnp.concatenate([normed, spread], axis=1)

    pl.semaphore_wait(barrier, 3 + 2 * (planes - 1))

    def remote(source, target, send, recv, to_side, to_dev):
        return pltpu.make_async_remote_copy(
            src_ref=source,
            dst_ref=target,
            send_sem=send,
            recv_sem=recv,
            device_id=(to_side, to_dev),
            device_id_type=MESH,
        )

    def plane(k):
        return lax.rem(zi - k + planes, planes)

    part_a = pl.ds(0, half)
    part_b = pl.ds(half, wide - half)
    out_a = pl.ds(0, half)
    out_b = pl.ds(half, half)

    def send_z(k):
        peer = lax.rem(zi + k, planes) * 4 + column
        return remote(
            gathered.at[dev], gathered.at[dev], z_send.at[k], z_recv.at[k], side, peer
        )

    def send_x(k):
        block = gathered.at[plane(k) * 4 + column]
        return remote(block, block, x_send.at[k], x_recv.at[k], side, x_dev)

    def send_y(k):
        block = gathered.at[plane(k) * 4 + column]
        return remote(block, block, y_send.at[k], y_recv.at[k], side, y_dev)

    def send_da(k):
        block = gathered.at[plane(k) * 4 + x_col, :, part_a]
        return remote(block, block, da_send.at[k], da_recv.at[k], side, y_dev)

    def send_db(k):
        block = gathered.at[plane(k) * 4 + y_col, :, part_b]
        return remote(block, block, db_send.at[k], db_recv.at[k], side, x_dev)

    def send_ra(k):
        return remote(
            partial.at[k, d_col, :, out_a],
            diag_in.at[k, :, out_a],
            ra_send.at[k],
            ra_recv.at[k],
            side,
            x_dev,
        )

    def send_rb(k):
        return remote(
            partial.at[k, d_col, :, out_b],
            diag_in.at[k, :, out_b],
            rb_send.at[k],
            rb_recv.at[k],
            side,
            y_dev,
        )

    def send_rx(k):
        return remote(
            partial.at[k, x_col], x_in.at[k], rx_send.at[k], rx_recv.at[k], side, x_dev
        )

    def send_ry(k):
        return remote(
            partial.at[k, y_col], y_in.at[k], ry_send.at[k], ry_recv.at[k], side, y_dev
        )

    def send_rz(k, to_side):
        columns = pl.ds(pl.multiple_of(to_side * half, half), half)
        return remote(
            plane_sum.at[k, :, columns],
            z_in.at[k, side],
            rz_send.at[k, to_side],
            rz_recv.at[k, side],
            to_side,
            plane(k) * 4 + column,
        )

    def wait_rz(k, from_side):
        columns = pl.ds(pl.multiple_of(side * half, half), half)
        remote(
            plane_sum.at[k, :, columns],
            z_in.at[k, from_side],
            rz_send.at[k, side],
            rz_recv.at[k, from_side],
            side,
            lax.rem(zi + k, planes) * 4 + column,
        ).wait_recv()

    send_x(0).start()
    send_y(0).start()
    for k in range(1, planes):
        send_z(k).start()

    def relay(k):
        send_z(k).wait_recv()
        send_x(k).start()
        send_y(k).start()

    def forward(k):
        send_x(k).wait_recv()
        send_da(k).start()
        send_y(k).wait_recv()
        send_db(k).start()

    def serve(k):
        send_da(k).wait_recv()
        send_db(k).wait_recv()
        at = pl.ds(pl.multiple_of(plane(k) * 4, 4), 4)
        block = gathered[at].reshape(4 * rows, wide)
        taken = block[:, :width]
        shares = dot(block[:, width:], select[...])
        inners = []
        for i in range(local):
            gate_part = dot(taken, gate_weight[i])
            up_part = dot(taken, up_weight[i])
            weight = shares[:, i * hidden_units : (i + 1) * hidden_units]
            inners.append((gate_part * sigmoid(gate_part) * up_part * weight).astype(BF16))
        inner_all = jnp.concatenate(inners, axis=1)
        down = down_weight[...].reshape(local * hidden_units, width)
        result = dot(inner_all, down).astype(BF16)
        partial[k] = result.reshape(4, rows, width)
        send_ra(k).start()
        send_rb(k).start()

    def reduce_diag(k):
        send_ra(k).wait_recv()
        partial[k, y_col, :, :half] = (
            partial[k, y_col, :, :half].astype(F32) + diag_in[k, :, :half].astype(F32)
        ).astype(BF16)
        send_ry(k).start()
        send_rb(k).wait_recv()
        partial[k, x_col, :, half:] = (
            partial[k, x_col, :, half:].astype(F32) + diag_in[k, :, half:].astype(F32)
        ).astype(BF16)
        send_rx(k).start()

    def reduce_plane(k):
        send_rx(k).wait_recv()
        send_ry(k).wait_recv()
        summed = (
            partial[k, column].astype(F32) + x_in[k].astype(F32) + y_in[k].astype(F32)
        )

        @pl.when(k > 0)
        def _():
            plane_sum[k] = summed.astype(BF16)
            send_rz(k, 0).start()
            send_rz(k, 1).start()

        @pl.when(k == 0)
        def _():
            base[...] = base[...] + summed
            base_out[...] = base[:, pl.ds(pl.multiple_of(other * half, half), half)]
            send_base().start()

    def send_base():
        return remote(base_out, base_in, side_sem.at[0], side_sem.at[1], other, dev)

    forward(0)
    if planes > 1:
        relay(1)

    for copy in shared_loads:
        copy.wait()
    gate_val = dot(normed, shared_gate[...])
    up_val = dot(normed, shared_up[...])
    inner = (gate_val * sigmoid(gate_val) * up_val).astype(BF16)
    mix_rows = shared_mix[...].astype(F32)
    mix_row = jnp.concatenate([mix_rows[i : i + 1] for i in range(mix_rows.shape[0])], axis=1)
    mix = jnp.sum(normed.astype(F32) * mix_row, axis=1, keepdims=True)
    base[...] = hidden + sigmoid(mix) * dot(inner, shared_down[...])

    for copy in expert_loads:
        copy.wait()

    def turn(k, carry):
        @pl.when(k + 2 < planes)
        def _():
            relay(k + 2)

        @pl.when(k + 1 < planes)
        def _():
            forward(k + 1)

        @pl.when(k < planes)
        def _():
            serve(k)

        @pl.when((k >= 1) & (k <= planes))
        def _():
            reduce_diag(k - 1)

        @pl.when(k >= 2)
        def _():
            reduce_plane(k - 2)

        return carry

    lax.fori_loop(0, planes + 2, turn, 0)

    send_base().wait_recv()
    own_rows = base[:, pl.ds(pl.multiple_of(side * half, half), half)]
    other_rows = base_in[...]
    for k in range(1, planes):
        wait_rz(k, side)
        own_rows = own_rows + z_in[k, side].astype(F32)
        wait_rz(k, other)
        other_rows = other_rows + z_in[k, other].astype(F32)
    out_ref[pl.ds(first, rows), :] = own_rows.astype(BF16)
    out_ref[pl.ds(pl.multiple_of(other * rows, rows), rows), :] = other_rows.astype(BF16)

    def drain(k, carry):
        for send in (send_x, send_y, send_da, send_db, send_ra, send_rb, send_rx, send_ry):
            send(k).wait_send()

        @pl.when(k > 0)
        def _():
            send_z(k).wait_send()
            send_rz(k, 0).wait_send()
            send_rz(k, 1).wait_send()

        return carry

    lax.fori_loop(0, planes, drain, 0)
    send_base().wait_send()


def on_device(
    out_gates,
    queries,
    keys_new,
    values_new,
    lengths,
    page_table,
    cache_pool,
    query_gain,
    key_gain,
    out_weight,
    residual,
    post_gain,
    experts,
    route_weights,
    gate_weight,
    up_weight,
    down_weight,
    shared_gate,
    shared_up,
    shared_down,
    shared_mix,
):
    n_dev = lax.axis_size("dev")
    planes = n_dev // 4
    rows_dev, width = residual.shape
    rows = rows_dev // 2
    half = width // 2
    local, _, hidden_units = gate_weight.shape
    terms = 2 * local * n_dev
    operands = (
        out_gates,
        queries,
        keys_new,
        values_new,
        lengths.reshape(1, -1),
        page_table.T,
        cache_pool,
        query_gain.reshape(1, -1),
        key_gain.reshape(1, -1),
        out_weight,
        residual,
        post_gain.reshape(1, -1),
        experts.T,
        route_weights.T,
        gate_weight,
        up_weight,
        down_weight,
        shared_gate,
        shared_up,
        shared_down,
        shared_mix.reshape(-1, 128),
    )
    by_row = (0, 1, 2, 3, 10)
    held = [
        pltpu.VMEM(((rows,) + value.shape[1:]) if i in by_row else value.shape, value.dtype)
        for i, value in enumerate(operands)
    ]
    loads = len(operands) - 4 + OUT_CHUNKS + 3 * local
    per_plane = pltpu.SemaphoreType.DMA((planes,))
    per_side = pltpu.SemaphoreType.DMA((planes, 2))
    flops = 2 * width * (
        width * rows + 3 * hidden_units * rows * (n_dev * local + 1)
    )
    return pl.pallas_call(
        functools.partial(kernel, planes),
        out_shape=jax.ShapeDtypeStruct((rows_dev, half), BF16),
        in_specs=[pl.BlockSpec(memory_space=pl.ANY)] * len(operands),
        out_specs=pl.BlockSpec(memory_space=pltpu.VMEM),
        scratch_shapes=held
        + [
            pltpu.VMEM((n_dev, rows, width + terms), BF16),
            pltpu.VMEM((terms, local * hidden_units), BF16),
            pltpu.VMEM((planes, 4, rows, width), BF16),
            pltpu.VMEM((planes, rows, width), BF16),
            pltpu.VMEM((planes, rows, width), BF16),
            pltpu.VMEM((planes, rows, width), BF16),
            pltpu.VMEM((planes, rows, width), BF16),
            pltpu.VMEM((planes, 2, rows, half), BF16),
            pltpu.VMEM((rows, width), F32),
            pltpu.VMEM((rows, half), F32),
            pltpu.VMEM((rows, half), F32),
            pltpu.SemaphoreType.DMA((loads,)),
        ]
        + [per_plane] * 18
        + [per_side] * 2
        + [pltpu.SemaphoreType.DMA((2,))],
        compiler_params=pltpu.CompilerParams(
            collective_id=0, has_side_effects=True, vmem_limit_bytes=56 * 1024 * 1024
        ),
        cost_estimate=pl.CostEstimate(
            flops=flops, bytes_accessed=27 * 1024 * 1024, transcendentals=1024 * 1024
        ),
    )(*operands)


def solution(mesh):
    placed = (
        P("dev", None),
        P("dev", None),
        P("dev", None),
        P("dev", None),
        P("dev"),
        P("dev", None),
        P("dev", None, None),
        P(),
        P(),
        P(),
        P("dev", None),
        P(),
        P("dev", None),
        P("dev", None),
        P("dev", None, None),
        P("dev", None, None),
        P("dev", None, None),
        P(),
        P(),
        P(),
        P(),
    )
    return jax.shard_map(
        on_device, mesh=mesh, in_specs=placed, out_specs=P("dev", "side"), check_vma=False
    )
```

```python
import functools

import jax
import jax.numpy as jnp
from jax import lax
from jax.experimental import pallas as pl
from jax.experimental.pallas import tpu as pltpu
from jax.sharding import PartitionSpec as P

eps = 1e-06
MESH = pl.DeviceIdType.MESH
F32 = jnp.float32
BF16 = jnp.bfloat16


def rms_scale(wide, gain):
    return wide * lax.rsqrt(jnp.mean(wide * wide, axis=-1, keepdims=True) + eps) * gain


def sigmoid(value):
    return 1.0 / (1.0 + jnp.exp(-value))


def dot(left, right):
    return jnp.dot(left, right, preferred_element_type=F32)


def quotient(value, by):
    if by & (by - 1) == 0:
        return lax.shift_right_logical(value, jnp.full_like(value, by.bit_length() - 1))
    return value // by


def remainder(value, by):
    if by & (by - 1) == 0:
        return value & (by - 1)
    return lax.rem(value, by)


OUT_CHUNKS = 4


def kernel(
    planes,
    gates_h,
    queries_h,
    keys_h,
    values_h,
    lengths_h,
    table_h,
    pool_h,
    query_gain_h,
    key_gain_h,
    out_weight_h,
    residual_h,
    post_gain_h,
    experts_h,
    route_h,
    gate_weight_h,
    up_weight_h,
    down_weight_h,
    shared_gate_h,
    shared_up_h,
    shared_down_h,
    shared_mix_h,
    out_ref,
    gates,
    queries,
    keys,
    values,
    lengths,
    table,
    pool,
    query_gain,
    key_gain,
    out_weight,
    residual,
    post_gain,
    experts,
    route,
    gate_weight,
    up_weight,
    down_weight,
    shared_gate,
    shared_up,
    shared_down,
    shared_mix,
    gathered,
    select,
    partial,
    diag_in,
    x_in,
    y_in,
    plane_sum,
    z_in,
    base,
    base_out,
    base_in,
    load_sem,
    z_send,
    z_recv,
    x_send,
    x_recv,
    y_send,
    y_recv,
    da_send,
    da_recv,
    db_send,
    db_recv,
    ra_send,
    ra_recv,
    rb_send,
    rb_recv,
    rx_send,
    rx_recv,
    ry_send,
    ry_recv,
    rz_send,
    rz_recv,
    side_sem,
):
    side = lax.axis_index("side")
    dev = lax.axis_index("dev")
    other = 1 - side
    column = lax.rem(dev, 4)
    zi = dev // 4
    x_bit = lax.rem(dev, 2)
    y_bit = lax.rem(dev // 2, 2)
    x_col = column + 1 - 2 * x_bit
    y_col = column + 2 - 4 * y_bit
    d_col = 3 - column
    x_dev = zi * 4 + x_col
    y_dev = zi * 4 + y_col

    rows = queries.shape[0]
    width = residual.shape[1]
    half = width // 2
    wide = gathered.shape[2]
    head_dim = keys.shape[1]
    heads = queries.shape[1] // head_dim
    first = pl.multiple_of(side * rows, rows)

    loads = []

    def load(source, target):
        copy = pltpu.make_async_copy(source, target, load_sem.at[len(loads)])
        copy.start()
        loads.append(copy)
        return copy

    mine = pl.ds(first, rows)
    small_loads = [
        load(queries_h.at[mine], queries),
        load(query_gain_h, query_gain),
        load(keys_h.at[mine], keys),
        load(key_gain_h, key_gain),
        load(lengths_h, lengths),
        load(table_h, table),
        load(experts_h, experts),
        load(route_h, route),
    ]
    pool_load = load(pool_h, pool)
    late_loads = [
        load(values_h.at[mine], values),
        load(gates_h.at[mine], gates),
        load(residual_h.at[mine], residual),
        load(post_gain_h, post_gain),
    ]
    step = out_weight.shape[0] // OUT_CHUNKS
    out_loads = [
        load(out_weight_h.at[pl.ds(i * step, step)], out_weight.at[pl.ds(i * step, step)])
        for i in range(OUT_CHUNKS)
    ]

    barrier = pltpu.get_barrier_semaphore()

    def greet(to_side, to_dev):
        pl.semaphore_signal(barrier, inc=1, device_id=(to_side, to_dev), device_id_type=MESH)

    greet(other, dev)
    greet(side, x_dev)
    greet(side, y_dev)
    for k in range(1, planes):
        peer = lax.rem(zi + k, planes) * 4 + column
        greet(side, peer)
        greet(other, peer)

    for copy in small_loads:
        copy.wait()

    lane_row = lax.broadcasted_iota(jnp.int32, (rows, lengths.shape[1]), 1)
    sub_row = lax.broadcasted_iota(jnp.int32, (rows, lengths.shape[1]), 0) + first
    picked = lane_row == sub_row

    def as_column(line):
        return jnp.sum(jnp.where(picked, line, jnp.zeros_like(line)), axis=1, keepdims=True)

    width_terms = wide - width
    experts_all = width_terms // 2
    route_val = route[...]
    share = route_val / jnp.sum(route_val, axis=0, keepdims=True)
    chosen = experts[...]
    place = lax.broadcasted_iota(jnp.int32, (rows, width_terms), 1)
    expert_at = remainder(place, experts_all)
    spread = jnp.zeros((rows, width_terms), F32)
    for k in range(experts.shape[0]):
        spread = spread + jnp.where(
            expert_at == as_column(chosen[k : k + 1]), as_column(share[k : k + 1]), 0.0
        )
    leading = spread.astype(BF16).astype(F32)
    spread = jnp.where(place < experts_all, leading, spread - leading).astype(BF16)

    tokens = pool.shape[0] * pool.shape[1]
    page = pool.shape[1]
    length_col = as_column(lengths[...])
    token = lax.broadcasted_iota(jnp.int32, (rows, tokens), 1)
    token_page = quotient(token, page)
    token_at = remainder(token, page)
    table_val = table[...]
    limit = jnp.zeros((rows, tokens), jnp.int32)
    for j in range(table.shape[0]):
        left = length_col - page * j
        named = jnp.where(left > 0, as_column(table_val[j : j + 1]), -1)
        limit = jnp.where(token_page == named, left, limit)
    valid = jnp.where(limit > token_at, 1.0, 0.0)
    valid = jnp.concatenate([valid] * heads, axis=0)

    def head(value, h):
        return value[:, h * head_dim : (h + 1) * head_dim]

    queries_val = queries[...].astype(F32)
    query_parts = [
        rms_scale(head(queries_val, h), query_gain[...]).astype(BF16) for h in range(heads)
    ]
    key_normed = rms_scale(keys[...].astype(F32), key_gain[...]).astype(BF16).astype(F32)
    own = jnp.concatenate(
        [jnp.sum(q.astype(F32) * key_normed, axis=1, keepdims=True) for q in query_parts], axis=0
    )
    query_all = jnp.concatenate(query_parts, axis=0)
    scale = head_dim ** (-0.5)
    pool_load.wait()
    cached_keys = pool[:, :, :head_dim].reshape(tokens, head_dim)
    scores = lax.dot_general(
        query_all, cached_keys, (((1,), (1,)), ((), ())), preferred_element_type=F32
    )
    weights = jnp.where(valid > 0.0, jnp.exp(scores * scale), 0.0)
    own_weight = jnp.exp(own * scale)
    total = jnp.sum(weights, axis=1, keepdims=True) + own_weight
    cached_values = pool[:, :, head_dim:].reshape(tokens, head_dim)
    mixed = dot(weights.astype(BF16), cached_values)
    for copy in late_loads:
        copy.wait()
    values_all = jnp.concatenate([values[...].astype(F32)] * heads, axis=0)
    mixed = (mixed + own_weight * values_all) / total
    attended = jnp.concatenate(
        [
            (
                mixed[h * rows : (h + 1) * rows]
                * sigmoid(gates[:, h * head_dim : (h + 1) * head_dim].astype(F32))
            ).astype(BF16)
            for h in range(heads)
        ],
        axis=1,
    )

    local = gate_weight.shape[0]
    hidden_units = gate_weight.shape[2]
    term = lax.broadcasted_iota(jnp.int32, (select.shape[0], 1), 0)
    unit = lax.broadcasted_iota(jnp.int32, (1, select.shape[1]), 1)
    wanted = dev * local + quotient(unit, hidden_units)
    select[...] = jnp.where(remainder(term, experts_all) == wanted, 1.0, 0.0).astype(BF16)

    shared_loads = [
        load(shared_gate_h, shared_gate),
        load(shared_up_h, shared_up),
        load(shared_down_h, shared_down),
        load(shared_mix_h, shared_mix),
    ]
    expert_loads = [
        load(source.at[i], target.at[i])
        for source, target in (
            (gate_weight_h, gate_weight),
            (up_weight_h, up_weight),
            (down_weight_h, down_weight),
        )
        for i in range(gate_weight.shape[0])
    ]
    projected = jnp.zeros((rows, width), F32)
    for i, copy in enumerate(out_loads):
        copy.wait()
        projected = projected + dot(
            attended[:, i * step : (i + 1) * step], out_weight[i * step : (i + 1) * step, :]
        )
    hidden = (residual[...].astype(F32) + projected).astype(BF16).astype(F32)
    normed = rms_scale(hidden, post_gain[...]).astype(BF16)

    gathered[dev] = jnp.concatenate([normed, spread], axis=1)

    pl.semaphore_wait(barrier, 3 + 2 * (planes - 1))

    def remote(source, target, send, recv, to_side, to_dev):
        return pltpu.make_async_remote_copy(
            src_ref=source,
            dst_ref=target,
            send_sem=send,
            recv_sem=recv,
            device_id=(to_side, to_dev),
            device_id_type=MESH,
        )

    def plane(k):
        return lax.rem(zi - k + planes, planes)

    part_a = pl.ds(0, half)
    part_b = pl.ds(half, wide - half)
    out_a = pl.ds(0, half)
    out_b = pl.ds(half, half)

    def send_z(k):
        peer = lax.rem(zi + k, planes) * 4 + column
        return remote(
            gathered.at[dev], gathered.at[dev], z_send.at[k], z_recv.at[k], side, peer
        )

    def send_x(k):
        block = gathered.at[plane(k) * 4 + column]
        return remote(block, block, x_send.at[k], x_recv.at[k], side, x_dev)

    def send_y(k):
        block = gathered.at[plane(k) * 4 + column]
        return remote(block, block, y_send.at[k], y_recv.at[k], side, y_dev)

    def send_da(k):
        block = gathered.at[plane(k) * 4 + x_col, :, part_a]
        return remote(block, block, da_send.at[k], da_recv.at[k], side, y_dev)

    def send_db(k):
        block = gathered.at[plane(k) * 4 + y_col, :, part_b]
        return remote(block, block, db_send.at[k], db_recv.at[k], side, x_dev)

    def send_ra(k):
        return remote(
            partial.at[k, d_col, :, out_a],
            diag_in.at[k, :, out_a],
            ra_send.at[k],
            ra_recv.at[k],
            side,
            x_dev,
        )

    def send_rb(k):
        return remote(
            partial.at[k, d_col, :, out_b],
            diag_in.at[k, :, out_b],
            rb_send.at[k],
            rb_recv.at[k],
            side,
            y_dev,
        )

    def send_rx(k):
        return remote(
            partial.at[k, x_col], x_in.at[k], rx_send.at[k], rx_recv.at[k], side, x_dev
        )

    def send_ry(k):
        return remote(
            partial.at[k, y_col], y_in.at[k], ry_send.at[k], ry_recv.at[k], side, y_dev
        )

    def send_rz(k, to_side):
        columns = pl.ds(pl.multiple_of(to_side * half, half), half)
        return remote(
            plane_sum.at[k, :, columns],
            z_in.at[k, side],
            rz_send.at[k, to_side],
            rz_recv.at[k, side],
            to_side,
            plane(k) * 4 + column,
        )

    def wait_rz(k, from_side):
        columns = pl.ds(pl.multiple_of(side * half, half), half)
        remote(
            plane_sum.at[k, :, columns],
            z_in.at[k, from_side],
            rz_send.at[k, side],
            rz_recv.at[k, from_side],
            side,
            lax.rem(zi + k, planes) * 4 + column,
        ).wait_recv()

    send_x(0).start()
    send_y(0).start()
    for k in range(1, planes):
        send_z(k).start()

    def relay(k):
        send_z(k).wait_recv()
        send_x(k).start()
        send_y(k).start()

    def forward(k):
        send_x(k).wait_recv()
        send_da(k).start()
        send_y(k).wait_recv()
        send_db(k).start()

    def serve(k):
        send_da(k).wait_recv()
        send_db(k).wait_recv()
        at = pl.ds(pl.multiple_of(plane(k) * 4, 4), 4)
        block = gathered[at].reshape(4 * rows, wide)
        taken = block[:, :width]
        shares = dot(block[:, width:], select[...])
        inners = []
        for i in range(local):
            gate_part = dot(taken, gate_weight[i])
            up_part = dot(taken, up_weight[i])
            weight = shares[:, i * hidden_units : (i + 1) * hidden_units]
            inners.append((gate_part * sigmoid(gate_part) * up_part * weight).astype(BF16))
        inner_all = jnp.concatenate(inners, axis=1)
        down = down_weight[...].reshape(local * hidden_units, width)
        result = dot(inner_all, down).astype(BF16)
        partial[k] = result.reshape(4, rows, width)

        @pl.when(k > 0)
        def _():
            send_ra(k).start()
            send_rb(k).start()

        @pl.when(k == planes - 1)
        def _():
            send_ra(0).start()
            send_rb(0).start()

    def reduce_diag(k):
        send_ra(k).wait_recv()
        partial[k, y_col, :, :half] = (
            partial[k, y_col, :, :half].astype(F32) + diag_in[k, :, :half].astype(F32)
        ).astype(BF16)
        send_ry(k).start()
        send_rb(k).wait_recv()
        partial[k, x_col, :, half:] = (
            partial[k, x_col, :, half:].astype(F32) + diag_in[k, :, half:].astype(F32)
        ).astype(BF16)
        send_rx(k).start()

    def reduce_plane(k):
        send_rx(k).wait_recv()
        send_ry(k).wait_recv()
        summed = (
            partial[k, column].astype(F32) + x_in[k].astype(F32) + y_in[k].astype(F32)
        )

        @pl.when(k > 0)
        def _():
            plane_sum[k] = summed.astype(BF16)
            send_rz(k, 0).start()
            send_rz(k, 1).start()

        @pl.when(k == 0)
        def _():
            base[...] = base[...] + summed
            base_out[...] = base[:, pl.ds(pl.multiple_of(other * half, half), half)]
            send_base().start()

    def send_base():
        return remote(base_out, base_in, side_sem.at[0], side_sem.at[1], other, dev)

    forward(0)
    if planes > 1:
        relay(1)

    for copy in shared_loads:
        copy.wait()
    gate_val = dot(normed, shared_gate[...])
    up_val = dot(normed, shared_up[...])
    inner = (gate_val * sigmoid(gate_val) * up_val).astype(BF16)
    mix_rows = shared_mix[...].astype(F32)
    mix_row = jnp.concatenate([mix_rows[i : i + 1] for i in range(mix_rows.shape[0])], axis=1)
    mix = jnp.sum(normed.astype(F32) * mix_row, axis=1, keepdims=True)
    base[...] = hidden + sigmoid(mix) * dot(inner, shared_down[...])

    for copy in expert_loads:
        copy.wait()

    def turn(k, carry):
        @pl.when(k + 2 < planes)
        def _():
            relay(k + 2)

        @pl.when(k + 1 < planes)
        def _():
            forward(k + 1)

        @pl.when(k < planes)
        def _():
            serve(k)

        @pl.when((k >= 2) & (k <= planes + 1))
        def _():
            reduce_diag(lax.rem(k - 1, planes))

        @pl.when(k >= 3)
        def _():
            reduce_plane(lax.rem(k - 2, planes))

        return carry

    lax.fori_loop(0, planes + 3, turn, 0)

    send_base().wait_recv()
    own_rows = base[:, pl.ds(pl.multiple_of(side * half, half), half)]
    other_rows = base_in[...]
    for k in range(1, planes):
        wait_rz(k, side)
        own_rows = own_rows + z_in[k, side].astype(F32)
        wait_rz(k, other)
        other_rows = other_rows + z_in[k, other].astype(F32)
    out_ref[pl.ds(first, rows), :] = own_rows.astype(BF16)
    out_ref[pl.ds(pl.multiple_of(other * rows, rows), rows), :] = other_rows.astype(BF16)

    def drain(k, carry):
        for send in (send_x, send_y, send_da, send_db, send_ra, send_rb, send_rx, send_ry):
            send(k).wait_send()

        @pl.when(k > 0)
        def _():
            send_z(k).wait_send()
            send_rz(k, 0).wait_send()
            send_rz(k, 1).wait_send()

        return carry

    lax.fori_loop(0, planes, drain, 0)
    send_base().wait_send()


def on_device(
    out_gates,
    queries,
    keys_new,
    values_new,
    lengths,
    page_table,
    cache_pool,
    query_gain,
    key_gain,
    out_weight,
    residual,
    post_gain,
    experts,
    route_weights,
    gate_weight,
    up_weight,
    down_weight,
    shared_gate,
    shared_up,
    shared_down,
    shared_mix,
):
    n_dev = lax.axis_size("dev")
    planes = n_dev // 4
    rows_dev, width = residual.shape
    rows = rows_dev // 2
    half = width // 2
    local, _, hidden_units = gate_weight.shape
    terms = 2 * local * n_dev
    operands = (
        out_gates,
        queries,
        keys_new,
        values_new,
        lengths.reshape(1, -1),
        page_table.T,
        cache_pool,
        query_gain.reshape(1, -1),
        key_gain.reshape(1, -1),
        out_weight,
        residual,
        post_gain.reshape(1, -1),
        experts.T,
        route_weights.T,
        gate_weight,
        up_weight,
        down_weight,
        shared_gate,
        shared_up,
        shared_down,
        shared_mix.reshape(-1, 128),
    )
    by_row = (0, 1, 2, 3, 10)
    held = [
        pltpu.VMEM(((rows,) + value.shape[1:]) if i in by_row else value.shape, value.dtype)
        for i, value in enumerate(operands)
    ]
    loads = len(operands) - 4 + OUT_CHUNKS + 3 * local
    per_plane = pltpu.SemaphoreType.DMA((planes,))
    per_side = pltpu.SemaphoreType.DMA((planes, 2))
    flops = 2 * width * (
        width * rows + 3 * hidden_units * rows * (n_dev * local + 1)
    )
    return pl.pallas_call(
        functools.partial(kernel, planes),
        out_shape=jax.ShapeDtypeStruct((rows_dev, half), BF16),
        in_specs=[pl.BlockSpec(memory_space=pl.ANY)] * len(operands),
        out_specs=pl.BlockSpec(memory_space=pltpu.VMEM),
        scratch_shapes=held
        + [
            pltpu.VMEM((n_dev, rows, width + terms), BF16),
            pltpu.VMEM((terms, local * hidden_units), BF16),
            pltpu.VMEM((planes, 4, rows, width), BF16),
            pltpu.VMEM((planes, rows, width), BF16),
            pltpu.VMEM((planes, rows, width), BF16),
            pltpu.VMEM((planes, rows, width), BF16),
            pltpu.VMEM((planes, rows, width), BF16),
            pltpu.VMEM((planes, 2, rows, half), BF16),
            pltpu.VMEM((rows, width), F32),
            pltpu.VMEM((rows, half), F32),
            pltpu.VMEM((rows, half), F32),
            pltpu.SemaphoreType.DMA((loads,)),
        ]
        + [per_plane] * 18
        + [per_side] * 2
        + [pltpu.SemaphoreType.DMA((2,))],
        compiler_params=pltpu.CompilerParams(
            collective_id=0, has_side_effects=True, vmem_limit_bytes=56 * 1024 * 1024
        ),
        cost_estimate=pl.CostEstimate(
            flops=flops, bytes_accessed=27 * 1024 * 1024, transcendentals=1024 * 1024
        ),
    )(*operands)


def solution(mesh):
    placed = (
        P("dev", None),
        P("dev", None),
        P("dev", None),
        P("dev", None),
        P("dev"),
        P("dev", None),
        P("dev", None, None),
        P(),
        P(),
        P(),
        P("dev", None),
        P(),
        P("dev", None),
        P("dev", None),
        P("dev", None, None),
        P("dev", None, None),
        P("dev", None, None),
        P(),
        P(),
        P(),
        P(),
    )
    return jax.shard_map(
        on_device, mesh=mesh, in_specs=placed, out_specs=P("dev", "side"), check_vma=False
    )
```
